256 devices in a mesh: row: 16 (over z_lo, x, core), col: 16 (over z_hi, y).
Axes of the slice: x: 4, y: 4, z: 8 (z_hi: 4, z_lo: 2; z = z_hi * 2 + z_lo), core: 2. Of those that a mesh axis runs over, the one named last changes fastest.
Arguments:
- tokens: bfloat16 [2048, 12288], P('row', 'col'), may hold values from -6 to 6
- up_weight: bfloat16 [12288, 24576], P('col', 'row'), may hold values from -0.15625 to 0.15625
- up_mask: int32 [96, 192], P('col', 'row'), may hold values from 0 to 1, as said below
- up_bias: float32 [24576], P('row'), may hold values from -3 to 3
- down_weight: bfloat16 [24576, 12288], P('row', 'col'), may hold values from -0.109375 to 0.109375
- down_mask: int32 [192, 96], P('row', 'col'), may hold values 0 or 1
- down_bias: float32 [12288], P('col'), may hold values from -3 to 3
Outputs:
- mixed: bfloat16 [2048, 12288], P('row', 'col')
The draws below stay inside these ranges and needn't reach their ends.
Inputs may be any that keep to these rules, and one draw needn't show every extreme that they name: Split up_mask into tiles of 12288 / (128 * 16) block rows by 24576 / (128 * 16) block columns, in the grid of the placement; every tile holds exactly one eighth of its entries as 1.
All inputs are finite; a program needn't handle non-finite values. No bound on the sum of `down_mask` on one device may be relied on, other than what follows from the above.
Results may differ from the reference program's by a relative error of at most 0.0044.
Values may be sent and summed in bfloat16 or wider, within the bound.
No kernel may reach another device: no remote copies, remote signals or barrier semaphores. Data moves between devices by JAX's collectives and lax.ppermute only.
A program may use at most 64 MiB of HBM per device.

```python
import jax
import jax.numpy as jnp

D = 12288
FF = 24576
BLOCK = 128
TOKENS = 2048
N_ROW = 16
N_COL = 16


def draw_up_mask(key, part):
    key = jax.random.fold_in(key, 11)
    tile_rows = D // (BLOCK * N_COL)
    tile_cols = FF // (BLOCK * N_ROW)
    cell_count = tile_rows * tile_cols
    keep_count = cell_count // 8
    tile_keys = jax.random.split(key, N_COL * N_ROW)
    orders = jax.vmap(lambda one_key: jax.random.permutation(one_key, cell_count))(tile_keys)
    tiles = (orders < keep_count).astype(jnp.int32).reshape(N_COL, N_ROW, tile_rows, tile_cols)
    return tiles.transpose(0, 2, 1, 3).reshape(N_COL * tile_rows, N_ROW * tile_cols)


def set_ends(array, stream_key, smallest, largest):
    spot = [jax.random.randint(jax.random.fold_in(stream_key, axis), (), 0, length) for axis, length in enumerate(array.shape)]
    longest = array.shape.index(max(array.shape))
    beside = spot[:longest] + [(spot[longest] + 1) % array.shape[longest]] + spot[longest + 1:]
    return array.at[tuple(spot)].set(smallest).at[tuple(beside)].set(largest)


def level_of(key, dims, shards, low, top_value):
    loudness, own = 1.0, jax.random.fold_in(key, 6)
    for position, shards_of in shards:
        draws = jnp.exp(jax.random.uniform(jax.random.fold_in(own, position), (shards_of,), jnp.float32, low / len(shards), top_value / len(shards)))
        loudness = loudness * jnp.repeat(draws, dims[position] // shards_of).reshape([-1 if axis == position else 1 for axis in range(len(dims))])
    return loudness


def scatter_about(stream_key, shape, spread, most, cuts=(), dtype=jnp.bfloat16):
    values = spread * jax.random.normal(stream_key, shape, jnp.float32)
    if cuts:
        values = values * level_of(stream_key, shape, cuts, -0.22, 0.18)
    return jnp.clip(values, -most, most).astype(dtype)


def setup_inputs(seed: int = 0) -> dict:
    keys = jax.random.split(jax.random.key(seed), 8)
    tokens = scatter_about(keys[0], (TOKENS, D), 1.0, 6.0, ((0, 16), (1, 16)))
    up_weight = scatter_about(keys[1], (D, FF), (D // 8) ** -0.5, 0.15625, ((0, 16), (1, 16)))
    up_mask = draw_up_mask(jax.random.fold_in(keys[7], 71), 0)
    up_bias = scatter_about(keys[3], (FF,), 0.5, 3.0, ((0, 16),), jnp.float32)
    down_weight = scatter_about(keys[4], (FF, D), (FF // 8) ** -0.5, 0.109375, ((0, 16), (1, 16)))
    down_mask = set_ends((jax.random.randint(keys[5], (FF // BLOCK, D // BLOCK), 0, 8) < 1).astype(jnp.int32), jax.random.fold_in(keys[5], 1), 0, 1)
    down_bias = scatter_about(keys[6], (D,), 0.5, 3.0, ((0, 16),), jnp.float32)
    return {"tokens": tokens, "up_weight": up_weight, "up_mask": up_mask, "up_bias": up_bias, "down_weight": down_weight, "down_mask": down_mask, "down_bias": down_bias}


def expand_mask(mask, weight):
    rows, cols = mask.shape
    side = weight.shape[0] // rows
    full = jnp.broadcast_to(mask[:, None, :, None], (rows, side, cols, side)).reshape(weight.shape)
    return jnp.where(full > 0, weight, jnp.zeros_like(weight))


def reference(tokens, up_weight, up_mask, up_bias, down_weight, down_mask, down_bias):
    up_kept = expand_mask(up_mask, up_weight)
    down_kept = expand_mask(down_mask, down_weight)
    pre = jnp.dot(tokens, up_kept, preferred_element_type=jnp.float32) + up_bias[None, :]
    hidden = jnp.maximum(pre, 0.0).astype(jnp.bfloat16)
    out = jnp.dot(hidden, down_kept, preferred_element_type=jnp.float32) + down_bias[None, :]
    return out.astype(jnp.bfloat16)
```

```python
import functools
import itertools

import jax
import jax.numpy as jnp
from jax import lax
from jax.experimental import pallas as pl
from jax.experimental.pallas import tpu as pltpu
from jax.sharding import Mesh
from jax.sharding import PartitionSpec as P

AXES = ("zl", "x", "core", "zh", "y")
SIZES = (2, 4, 2, 4, 4)
ROW = ("zl", "x", "core")
COL = ("zh", "y")
BLOCK = 128
UP_KEPT = 9
PAIR = 18
VMEM_LIMIT = 50 * 1024 * 1024
bf16 = jnp.bfloat16
f32 = jnp.float32


def flat(coords):
    at = 0
    for value, size in zip(coords, SIZES):
        at = at * size + value
    return at


def route(move):
    pairs = []
    for coords in itertools.product(*[range(size) for size in SIZES]):
        named = dict(zip(AXES, coords))
        named.update(move(**named))
        pairs.append((flat(coords), flat([named[axis] for axis in AXES])))
    return pairs


def flip(axis, mask):
    return route(lambda **at: {axis: at[axis] ^ mask})


def send(array, pairs):
    return lax.ppermute(array, AXES, pairs)


def expand_mask(mask, weight):
    rows, cols = mask.shape
    side = weight.shape[0] // rows
    full = jnp.broadcast_to(mask[:, None, :, None], (rows, side, cols, side)).reshape(weight.shape)
    return jnp.where(full > 0, weight, jnp.zeros_like(weight))


def together(*trees):
    return lax.optimization_barrier(trees)


def first_half(array):
    return array[: array.shape[0] // 2]


def last_half(array):
    return array[array.shape[0] // 2 :]


def swap_core(array):
    return send(array, flip("core", 1))


def ring_first(array, axis):
    return send(array, flip(axis, 1)), send(array, flip(axis, 3))


def ring_second(near, far, axis):
    return send(first_half(near), flip(axis, 3)), send(last_half(far), flip(axis, 1))


def sum_first(to_near, to_far, axis):
    return send(to_near, flip(axis, 1)), send(to_far, flip(axis, 3))


def sum_second(near, far, keep, axis):
    last = send((near[1].astype(f32) + keep[2]).astype(bf16), flip(axis, 3))
    first = send((far[1].astype(f32) + keep[3]).astype(bf16), flip(axis, 1))
    return last, first


def summed(keep, near, far, last, first):
    return keep[0] + near[0].astype(f32) + last.astype(f32), keep[1] + far[0].astype(f32) + first.astype(f32)


def write_notes(out, notes, lane, last, kept, down_kept):
    note = jnp.where(lane == BLOCK - 1, kept.astype(f32), notes[...])
    note = jnp.where(lane == BLOCK - 2, down_kept.astype(f32), note).astype(bf16)
    for copy in range(4):
        out[copy, last] = note


def kept_in(mask_ref):
    return jnp.sum((mask_ref[...] > 0).astype(f32)).astype(jnp.int32)


def pack_up_kernel(mask_ref, down_mask_ref, w_ref, out, notes, found):
    lane = lax.broadcasted_iota(jnp.int32, (16, BLOCK), 1)
    notes[...] = jnp.zeros_like(notes)
    found[0] = 0
    for i, j in itertools.product(range(6), range(12)):

        @pl.when(mask_ref[i, j] > 0)
        def _(i=i, j=j):
            b = found[0]
            found[0] = b + 1
            notes[...] = jnp.where(lane == b, float(12 * i + j), notes[...])
            block = w_ref[i * BLOCK : (i + 1) * BLOCK, j * BLOCK : (j + 1) * BLOCK].reshape(8, 16, BLOCK)
            for copy in range(4):
                out[copy, pl.ds(8 * b, 8)] = block

    write_notes(out, notes, lane, 8 * UP_KEPT, found[0], kept_in(down_mask_ref))


def pack_down_kernel(at_ref, mask_ref, other_mask_ref, mask_v, other_mask_v, w_ref, other_ref, out, notes, found):
    lane = lax.broadcasted_iota(jnp.int32, (16, BLOCK), 1)
    out[...] = jnp.zeros_like(out)
    notes[...] = jnp.zeros_like(notes)
    core = at_ref[2]
    mine, other = kept_in(mask_v), kept_in(other_mask_v)
    found[0] = jnp.where(core == 0, 0, other - PAIR)
    found[1] = jnp.where(core == 0, mine, -PAIR)
    for n, (mask, weight) in enumerate(((mask_ref, w_ref), (other_mask_ref, other_ref))):
        name = 72 * (core ^ n)
        for i, j in itertools.product(range(12), range(6)):

            @pl.when(mask[i, j] > 0)
            def _(i=i, j=j, n=n, name=name, weight=weight):
                b = found[n]
                found[n] = b + 1

                @pl.when((b >= 0) & (b < PAIR))
                def _():
                    notes[...] = jnp.where(lane == b, (name + 6 * i + j).astype(f32), notes[...])
                    block = weight[i * BLOCK : (i + 1) * BLOCK, j * BLOCK : (j + 1) * BLOCK].reshape(8, 16, BLOCK)
                    for copy in range(4):
                        out[copy, pl.ds(8 * b, 8)] = block

    kept = jnp.clip(mine + other - PAIR * core, 0, PAIR)
    write_notes(out, notes, lane, 8 * PAIR, kept, mine)


def pack(kernel, cap, *args):
    smem = pl.BlockSpec(memory_space=pltpu.SMEM)
    vmem = pl.BlockSpec(memory_space=pltpu.VMEM)
    return pl.pallas_call(
        kernel,
        out_shape=jax.ShapeDtypeStruct((4, 8 * cap + 1, 16, BLOCK), bf16),
        in_specs=[smem, vmem, vmem] if kernel is pack_up_kernel else [smem] * 3 + [vmem] * 4,
        out_specs=vmem,
        scratch_shapes=[pltpu.VMEM((16, BLOCK), f32), pltpu.SMEM((2,), jnp.int32)],
        compiler_params=pltpu.CompilerParams(vmem_limit_bytes=VMEM_LIMIT),
    )(*args)


def spread(array, axis="zh"):
    return lax.all_to_all(array, axis, split_axis=0, concat_axis=0, tiled=True)


def notes_of(mine, other, cap):
    return jnp.stack([mine[:, 8 * cap, 0], other[:, 8 * cap, 0]]).astype(jnp.int32)


def up_kernel(at_ref, note_ref, *refs):
    weights, tokens, (to_near, to_far, keep) = refs[:2], refs[2:7], refs[7:10]
    acts, acc0, acc1, sems = refs[10:]
    y = at_ref[4]
    copies = []
    for p, s, source in itertools.product(range(4), range(2), range(4)):
        part = tokens[p].at[source, s] if p < 3 else tokens[3 + source // 2].at[source % 2, s]
        copies.append(pltpu.make_async_copy(part, acts.at[source, s, p], sems.at[8 * p + 4 * s + source]))
    for copy in copies:
        copy.start()
    accs = (acc0, acc1)
    for acc in accs:
        acc[...] = jnp.zeros_like(acc)
    for copy in copies:
        copy.wait()
    for source in range(4):

        def step(group, _):
            sums = []
            for n, side in itertools.product(range(3), range(2)):
                b = 3 * group + n
                cell = note_ref[side, source, b]
                i, c = cell // 12, cell % 12
                left = pl.multiple_of(i * BLOCK, BLOCK)
                block = weights[side][source, pl.ds(8 * b, 8)].reshape(BLOCK, BLOCK)
                some = acts[source, :, :, :, pl.ds(left, BLOCK)].reshape(2 * BLOCK, BLOCK)
                sums.append((side, c, jnp.dot(some, block, preferred_element_type=f32)))
            for side, c, more in sums:
                accs[side][c] += more
            return 0

        lax.fori_loop(0, UP_KEPT // 3, step, 0)

    def write(ref, n, side, mask):
        top = pl.multiple_of((y ^ mask) * 64, 64)
        for c in range(12):
            ref[n, :, c * BLOCK : (c + 1) * BLOCK] = accs[side][c, pl.ds(top, 64), :].astype(ref.dtype)

    write(to_near, 0, 0, 1)
    write(to_near, 1, 0, 2)
    write(to_far, 0, 1, 3)
    write(to_far, 1, 1, 2)
    write(keep, 0, 0, 0)
    write(keep, 1, 1, 0)
    write(keep, 2, 0, 3)
    write(keep, 3, 1, 1)


def up(at, notes, weights, tokens):
    smem = pl.BlockSpec(memory_space=pltpu.SMEM)
    vmem = pl.BlockSpec(memory_space=pltpu.VMEM)
    hbm = pl.BlockSpec(memory_space=pl.ANY)
    return pl.pallas_call(
        up_kernel,
        out_shape=[
            jax.ShapeDtypeStruct((2, 64, 12 * BLOCK), bf16),
            jax.ShapeDtypeStruct((2, 64, 12 * BLOCK), bf16),
            jax.ShapeDtypeStruct((4, 64, 12 * BLOCK), f32),
        ],
        in_specs=[smem, smem, vmem, vmem] + [hbm] * 5,
        out_specs=[vmem] * 3,
        scratch_shapes=[
            pltpu.VMEM((4, 2, 4, 32, 6 * BLOCK), bf16),
            pltpu.VMEM((12, 2 * BLOCK, BLOCK), f32),
            pltpu.VMEM((12, 2 * BLOCK, BLOCK), f32),
            pltpu.SemaphoreType.DMA((32,)),
        ],
        compiler_params=pltpu.CompilerParams(vmem_limit_bytes=VMEM_LIMIT),
    )(at, notes, *weights, *tokens)


def down_kernel(at_ref, note_ref, *refs):
    weights, hidden, (to_near, to_far, keep) = refs[:2], refs[2:7], refs[7:10]
    acts, acc0, acc1, sems = refs[10:]
    core, y = at_ref[2], at_ref[4]
    copies = []
    for n, mask in enumerate((0, 1, 3, 2)):
        for side in range(2):
            part = hidden[n].at[side] if mask != 2 else hidden[3 + side].at[0]
            copies.append(pltpu.make_async_copy(part, acts.at[y ^ mask, side], sems.at[len(copies)]))
    for copy in copies:
        copy.start()
    accs = (acc0, acc1)
    for acc in accs:
        acc[...] = jnp.zeros_like(acc)
    for copy in copies:
        copy.wait()
    over = jnp.min(acts[:, 0, 0:16, 0:BLOCK].astype(f32)) < 0.0
    for source in range(4):

        def step(group, _):
            sums = []
            for n, side in itertools.product(range(3), range(2)):
                b = 3 * group + n
                name = note_ref[side, source, b]
                of = (name >= 72).astype(jnp.int32)
                cell = name - 72 * of
                i, c = cell // 6, cell % 6
                left = pl.multiple_of(i * BLOCK, BLOCK)
                block = weights[side][source, pl.ds(8 * b, 8)].reshape(BLOCK, BLOCK)
                some = acts[:, of ^ core, :, pl.ds(left, BLOCK)].reshape(2 * BLOCK, BLOCK)
                sums.append((side, source * 6 + c, jnp.dot(some, block, preferred_element_type=f32)))
            for side, c, more in sums:
                accs[side][c] += more
            return 0

        most = jnp.maximum(note_ref[0, source, BLOCK - 1], note_ref[1, source, BLOCK - 1])
        lax.fori_loop(0, (most + 2) // 3, step, 0)
    spoilt = jnp.where(over, jnp.nan, 0.0).astype(f32)

    def write(ref, n, half, p):
        top = half * BLOCK + 32 * p
        for target, c in itertools.product(range(4), range(6)):
            total = acc0[target * 6 + c, top : top + 32, :] + acc1[target * 6 + c, top : top + 32, :] + spoilt
            ref[n, target, :, c * BLOCK : (c + 1) * BLOCK] = total.astype(ref.dtype)

    write(to_near, 0, 0, 1)
    write(to_near, 1, 0, 3)
    write(to_far, 0, 1, 2)
    write(to_far, 1, 1, 3)
    write(keep, 0, 0, 0)
    write(keep, 1, 1, 0)
    write(keep, 2, 0, 2)
    write(keep, 3, 1, 1)


def down(at, notes, weights, hidden):
    smem = pl.BlockSpec(memory_space=pltpu.SMEM)
    vmem = pl.BlockSpec(memory_space=pltpu.VMEM)
    hbm = pl.BlockSpec(memory_space=pl.ANY)
    return pl.pallas_call(
        down_kernel,
        out_shape=[
            jax.ShapeDtypeStruct((2, 4, 32, 6 * BLOCK), bf16),
            jax.ShapeDtypeStruct((2, 4, 32, 6 * BLOCK), bf16),
            jax.ShapeDtypeStruct((4, 4, 32, 6 * BLOCK), f32),
        ],
        in_specs=[smem, smem, vmem, vmem] + [hbm] * 5,
        out_specs=[vmem] * 3,
        scratch_shapes=[
            pltpu.VMEM((4, 2, 64, 12 * BLOCK), bf16),
            pltpu.VMEM((24, 2 * BLOCK, BLOCK), f32),
            pltpu.VMEM((24, 2 * BLOCK, BLOCK), f32),
            pltpu.SemaphoreType.DMA((8,)),
        ],
        compiler_params=pltpu.CompilerParams(vmem_limit_bytes=VMEM_LIMIT),
    )(at, notes, *weights, *hidden)


def body(tokens, up_weight, up_mask, up_bias, down_weight, down_mask, down_bias):
    at = jnp.stack([lax.axis_index(axis) for axis in AXES]).astype(jnp.int32)

    z = ("zh", "zl")
    rows = tokens.reshape(4, 1, 32, 6 * BLOCK)
    own = spread(jnp.broadcast_to(rows, (4, 2, 32, 6 * BLOCK)).reshape(8, 32, 6 * BLOCK), z)
    own = own.reshape(4, 2, 32, 6 * BLOCK)
    up_packed = pack(pack_up_kernel, UP_KEPT, up_mask, down_mask, up_weight)
    biases = jnp.stack([up_bias, swap_core(up_bias)])
    other_down, other_mask = swap_core(down_weight), swap_core(down_mask)

    up_mine = spread(up_packed)
    near, far = ring_first(own, "x")
    down_packed = pack(
        pack_down_kernel, PAIR, at, down_mask, other_mask, down_mask, other_mask, down_weight, other_down
    )
    near, far, down_packed = together(near, far, down_packed)
    left, right = ring_second(near, far, "x")
    up_mine, left, right, down_packed, biases = together(up_mine, left, right, down_packed, biases)

    up_other = swap_core(up_mine)
    down_mine = spread(down_packed)
    up_notes = notes_of(up_mine, up_other, UP_KEPT)
    to_near, to_far, keep = up(at, up_notes, [up_mine, up_other], [own, near, far, left, right])

    near, far = sum_first(to_near, to_far, "y")
    near, far = together(near, far)
    last, first = sum_second(near, far, keep, "y")
    sums = jnp.stack(summed(keep, near, far, last, first))
    hidden = jnp.maximum(sums + biases[:, None, :], 0.0).astype(bf16)
    over = jnp.max(up_notes[0, :, BLOCK - 2] + up_notes[1, :, BLOCK - 2]) > 2 * PAIR
    marked = jnp.where(over, -jnp.ones_like(hidden), hidden)
    near, far = ring_first(marked, "y")
    near, far = together(near, far)
    left, right = ring_second(near, far, "y")
    left, right, down_mine = together(left, right, down_mine)

    down_other = swap_core(down_mine)
    down_notes = notes_of(down_mine, down_other, PAIR)
    to_near, to_far, keep = down(at, down_notes, [down_mine, down_other], [marked, near, far, left, right])

    def place(*sums):
        pieces = jnp.stack(sums, axis=1).astype(bf16).reshape(8, 32, 6 * BLOCK)
        got = spread(pieces, z).reshape(4, 2, 32, 6 * BLOCK).astype(f32)
        return (got[:, 0] + got[:, 1] + down_bias).astype(bf16).reshape(BLOCK, 6 * BLOCK)

    near, far = sum_first(to_near, to_far, "x")
    last, first = sum_second(near, far, keep, "x")
    out = place(*summed(keep, near, far, last, first))

    def whole(_):
        kept = lax.all_gather(expand_mask(down_mask, down_weight), "zh")
        kept = jnp.stack([kept, swap_core(kept)]).transpose(0, 2, 1, 3).reshape(24 * BLOCK, 24 * BLOCK)
        acts = lax.all_gather(hidden, "y").transpose(0, 2, 1, 3).reshape(2 * BLOCK, 24 * BLOCK)
        sums = jnp.dot(acts, kept, preferred_element_type=f32).reshape(2, 4, 32, 4, 6 * BLOCK)
        x = lax.axis_index("x")
        order = jnp.array([0, 1, 3, 2])[x ^ jnp.arange(4)]
        sums = lax.psum(jnp.take(sums, order, axis=1), "x")
        sums = lax.dynamic_index_in_dim(sums, x, 1, keepdims=False).transpose(0, 2, 1, 3)
        return place(sums[0], sums[1])

    return lax.cond(jnp.isnan(out[0, 0]), whole, lambda _: out, 0)


def solution(mesh):
    fine = Mesh(mesh.devices.reshape(SIZES), AXES)
    in_specs = (P(ROW, COL), P(COL, ROW), P(COL, ROW), P(ROW), P(ROW, COL), P(ROW, COL), P(COL))
    return jax.shard_map(body, mesh=fine, in_specs=in_specs, out_specs=P(ROW, COL), check_vma=False)
```

```python
import functools
import itertools

import jax
import jax.numpy as jnp
from jax import lax
from jax.experimental import pallas as pl
from jax.experimental.pallas import tpu as pltpu
from jax.sharding import Mesh
from jax.sharding import PartitionSpec as P

AXES = ("zl", "x", "core", "zh", "y")
SIZES = (2, 4, 2, 4, 4)
ROW = ("zl", "x", "core")
COL = ("zh", "y")
BLOCK = 128
UP_KEPT = 9
PAIR = 18
VMEM_LIMIT = 50 * 1024 * 1024
DOWN_LIMIT = 40 * 1024 * 1024
bf16 = jnp.bfloat16
f32 = jnp.float32


def flat(coords):
    at = 0
    for value, size in zip(coords, SIZES):
        at = at * size + value
    return at


def route(move):
    pairs = []
    for coords in itertools.product(*[range(size) for size in SIZES]):
        named = dict(zip(AXES, coords))
        named.update(move(**named))
        pairs.append((flat(coords), flat([named[axis] for axis in AXES])))
    return pairs


def flip(axis, mask):
    return route(lambda **at: {axis: at[axis] ^ mask})


def send(array, pairs):
    return lax.ppermute(array, AXES, pairs)


def expand_mask(mask, weight):
    rows, cols = mask.shape
    side = weight.shape[0] // rows
    full = jnp.broadcast_to(mask[:, None, :, None], (rows, side, cols, side)).reshape(weight.shape)
    return jnp.where(full > 0, weight, jnp.zeros_like(weight))


def together(*trees):
    return lax.optimization_barrier(trees)


def first_half(array):
    return array[: array.shape[0] // 2]


def last_half(array):
    return array[array.shape[0] // 2 :]


def swap_core(array):
    return send(array, flip("core", 1))


def ring_first(array, axis):
    return send(array, flip(axis, 1)), send(array, flip(axis, 3))


def ring_second(near, far, axis):
    return send(first_half(near), flip(axis, 3)), send(last_half(far), flip(axis, 1))


def sum_first(to_near, to_far, axis):
    return send(to_near, flip(axis, 1)), send(to_far, flip(axis, 3))


def sum_second(near, far, keep, axis):
    last = send((near[1].astype(f32) + keep[2]).astype(bf16), flip(axis, 3))
    first = send((far[1].astype(f32) + keep[3]).astype(bf16), flip(axis, 1))
    return last, first


def summed(keep, near, far, last, first):
    return keep[0] + near[0].astype(f32) + last.astype(f32), keep[1] + far[0].astype(f32) + first.astype(f32)


def write_notes(out, notes, lane, last, kept, down_kept):
    note = jnp.where(lane == BLOCK - 1, kept.astype(f32), notes[...])
    note = jnp.where(lane == BLOCK - 2, down_kept.astype(f32), note).astype(bf16)
    if len(out.shape) == 3:
        out[last] = note
    else:
        for copy in range(4):
            out[copy, last] = note


def kept_in(mask_ref):
    return jnp.sum((mask_ref[...] > 0).astype(f32)).astype(jnp.int32)


def pack_up_kernel(mask_ref, down_mask_ref, w_ref, out, notes, blocks, found, sems):
    lane = lax.broadcasted_iota(jnp.int32, (16, BLOCK), 1)
    notes[...] = jnp.zeros_like(notes)
    found[0] = 0

    def fetch(i, j, b):
        block = w_ref.at[pl.ds(i * BLOCK, BLOCK), pl.ds(j * BLOCK, BLOCK)]
        return pltpu.make_async_copy(block, blocks.at[b], sems.at[b])

    for i, j in itertools.product(range(6), range(12)):

        @pl.when(mask_ref[i, j] > 0)
        def _(i=i, j=j):
            b = found[0]
            found[0] = b + 1
            fetch(i, j, b).start()
            notes[...] = jnp.where(lane == b, float(12 * i + j), notes[...])

    write_notes(out, notes, lane, 8 * UP_KEPT, found[0], kept_in(down_mask_ref))
    for b in range(UP_KEPT):
        fetch(0, 0, b).wait()
        out[8 * b : 8 * b + 8] = blocks[b].reshape(8, 16, BLOCK)


def pack_down_kernel(at_ref, mask_ref, other_mask_ref, mask_v, other_mask_v, w_ref, other_ref, out, notes, found):
    lane = lax.broadcasted_iota(jnp.int32, (16, BLOCK), 1)
    out[...] = jnp.zeros_like(out)
    notes[...] = jnp.zeros_like(notes)
    core = at_ref[2]
    mine, other = kept_in(mask_v), kept_in(other_mask_v)
    found[0] = jnp.where(core == 0, 0, other - PAIR)
    found[1] = jnp.where(core == 0, mine, -PAIR)
    for n, (mask, weight) in enumerate(((mask_ref, w_ref), (other_mask_ref, other_ref))):
        name = 72 * (core ^ n)
        for i, j in itertools.product(range(12), range(6)):

            @pl.when(mask[i, j] > 0)
            def _(i=i, j=j, n=n, name=name, weight=weight):
                b = found[n]
                found[n] = b + 1

                @pl.when((b >= 0) & (b < PAIR))
                def _():
                    notes[...] = jnp.where(lane == b, (name + 6 * i + j).astype(f32), notes[...])
                    block = weight[i * BLOCK : (i + 1) * BLOCK, j * BLOCK : (j + 1) * BLOCK].reshape(8, 16, BLOCK)
                    for copy in range(4):
                        out[copy, pl.ds(8 * b, 8)] = block

    kept = jnp.clip(mine + other - PAIR * core, 0, PAIR)
    write_notes(out, notes, lane, 8 * PAIR, kept, mine)


def pack_up(mask, down_mask, weight):
    vmem = pl.BlockSpec(memory_space=pltpu.VMEM)
    return pl.pallas_call(
        pack_up_kernel,
        out_shape=jax.ShapeDtypeStruct((8 * UP_KEPT + 1, 16, BLOCK), bf16),
        in_specs=[pl.BlockSpec(memory_space=pltpu.SMEM), vmem, pl.BlockSpec(memory_space=pltpu.HBM)],
        out_specs=vmem,
        scratch_shapes=[
            pltpu.VMEM((16, BLOCK), f32),
            pltpu.VMEM((UP_KEPT, BLOCK, BLOCK), bf16),
            pltpu.SMEM((1,), jnp.int32),
            pltpu.SemaphoreType.DMA((UP_KEPT,)),
        ],
        compiler_params=pltpu.CompilerParams(vmem_limit_bytes=VMEM_LIMIT),
    )(mask, down_mask, weight)


def pack_down(*args):
    smem = pl.BlockSpec(memory_space=pltpu.SMEM)
    vmem = pl.BlockSpec(memory_space=pltpu.VMEM)
    return pl.pallas_call(
        pack_down_kernel,
        out_shape=jax.ShapeDtypeStruct((4, 8 * PAIR + 1, 16, BLOCK), bf16),
        in_specs=[smem] * 3 + [vmem] * 4,
        out_specs=vmem,
        scratch_shapes=[pltpu.VMEM((16, BLOCK), f32), pltpu.SMEM((2,), jnp.int32)],
        compiler_params=pltpu.CompilerParams(vmem_limit_bytes=VMEM_LIMIT),
    )(*args)


def spread(array, axis="zh"):
    return lax.all_to_all(array, axis, split_axis=0, concat_axis=0, tiled=True)


def read_notes(rows, staged, note_ref, sem):
    for n, row in enumerate(rows):
        staged[n : n + 1] = row.astype(f32).astype(jnp.int32)
    copy = pltpu.make_async_copy(staged, note_ref, sem)
    copy.start()
    copy.wait()


def notes(rows):
    return [pltpu.VMEM((rows, BLOCK), jnp.int32), pltpu.SMEM((rows, BLOCK), jnp.int32), pltpu.SemaphoreType.DMA]


def up_kernel(at_ref, *refs):
    weights, tokens, (to_near, to_far, keep) = (refs[:4], refs[4:8]), refs[8:13], refs[13:16]
    flag, acts, acc0, acc1, sems, staged, note_ref, note_sem = refs[16:]
    zh, y = at_ref[3], at_ref[4]
    copies = []
    for p, s, source in itertools.product(range(4), range(2), range(4)):
        part = tokens[p].at[source, s] if p < 3 else tokens[3 + source // 2].at[source % 2, s]
        copies.append(pltpu.make_async_copy(part, acts.at[source, s, p], sems.at[8 * p + 4 * s + source]))
    for copy in copies:
        copy.start()
    read_notes([pack[8 * UP_KEPT, 0:1] for pack in refs[:8]], staged, note_ref, note_sem)
    most = note_ref[0, BLOCK - 2] + note_ref[4, BLOCK - 2]
    for p in range(1, 4):
        most = jnp.maximum(most, note_ref[p, BLOCK - 2] + note_ref[4 + p, BLOCK - 2])
    flag[...] = jnp.full_like(flag, jnp.where(most > 2 * PAIR, 1.0, 0.0))
    accs = (acc0, acc1)
    for acc in accs:
        acc[...] = jnp.zeros_like(acc)
    for copy in copies:
        copy.wait()
    for p, mask in enumerate((0, 1, 3, 2)):
        sums = []
        for b, side in itertools.product(range(UP_KEPT), range(2)):
            cell = note_ref[4 * side + p, b]
            i, c = cell // 12, cell % 12
            left = pl.multiple_of(i * BLOCK, BLOCK)
            block = weights[side][p][8 * b : 8 * b + 8].reshape(BLOCK, BLOCK)
            some = acts[zh ^ mask, :, :, :, pl.ds(left, BLOCK)].reshape(2 * BLOCK, BLOCK)
            sums.append((side, c, jnp.dot(some, block, preferred_element_type=f32)))
        for side, c, more in sums:
            accs[side][c] += more

    def write(ref, n, side, mask):
        top = pl.multiple_of((y ^ mask) * 64, 64)
        for c in range(12):
            ref[n, :, c * BLOCK : (c + 1) * BLOCK] = accs[side][c, pl.ds(top, 64), :].astype(ref.dtype)

    write(to_near, 0, 0, 1)
    write(to_near, 1, 0, 2)
    write(to_far, 0, 1, 3)
    write(to_far, 1, 1, 2)
    write(keep, 0, 0, 0)
    write(keep, 1, 1, 0)
    write(keep, 2, 0, 3)
    write(keep, 3, 1, 1)


def up(at, weights, tokens):
    smem = pl.BlockSpec(memory_space=pltpu.SMEM)
    vmem = pl.BlockSpec(memory_space=pltpu.VMEM)
    hbm = pl.BlockSpec(memory_space=pl.ANY)
    return pl.pallas_call(
        up_kernel,
        out_shape=[
            jax.ShapeDtypeStruct((2, 64, 12 * BLOCK), bf16),
            jax.ShapeDtypeStruct((2, 64, 12 * BLOCK), bf16),
            jax.ShapeDtypeStruct((4, 64, 12 * BLOCK), f32),
            jax.ShapeDtypeStruct((8, BLOCK), f32),
        ],
        in_specs=[smem] + [vmem] * 8 + [hbm] * 5,
        out_specs=[vmem] * 4,
        scratch_shapes=[
            pltpu.VMEM((4, 2, 4, 32, 6 * BLOCK), bf16),
            pltpu.VMEM((12, 2 * BLOCK, BLOCK), f32),
            pltpu.VMEM((12, 2 * BLOCK, BLOCK), f32),
            pltpu.SemaphoreType.DMA((32,)),
            *notes(8),
        ],
        compiler_params=pltpu.CompilerParams(vmem_limit_bytes=VMEM_LIMIT),
    )(at, *weights, *tokens)


def down_kernel(last, at_ref, *refs):
    packs, hidden = refs[0], refs[1:6]
    if last:
        before, to_near, to_far, keep = refs[6:10]
        acts, acc, sems, staged, note_ref, note_sem = refs[10:]
    else:
        acc = refs[6]
        acts, sems, staged, note_ref, note_sem = refs[7:]
    core, y = at_ref[2], at_ref[4]
    copies = []
    for n, mask in enumerate((0, 1, 3, 2)):
        for side in range(2):
            part = hidden[n].at[side] if mask != 2 else hidden[3 + side].at[0]
            copies.append(pltpu.make_async_copy(part, acts.at[y ^ mask, side], sems.at[2 * n + side]))
    for copy in copies:
        copy.start()
    read_notes([packs[source, 8 * PAIR, 0:1] for source in range(4)], staged, note_ref, note_sem)
    acc[...] = jnp.zeros_like(acc)
    for copy in copies:
        copy.wait()
    for source in range(4):

        def step(group, _, source=source):
            sums = []
            for n in range(6):
                b = 6 * group + n
                name = note_ref[source, b]
                of = (name >= 72).astype(jnp.int32)
                cell = name - 72 * of
                i, c = cell // 6, cell % 6
                left = pl.multiple_of(i * BLOCK, BLOCK)
                block = packs[source, pl.ds(8 * b, 8)].reshape(BLOCK, BLOCK)
                some = acts[:, of ^ core, :, pl.ds(left, BLOCK)].reshape(2 * BLOCK, BLOCK)
                sums.append((source * 6 + c, jnp.dot(some, block, preferred_element_type=f32)))
            for c, more in sums:
                acc[c] += more
            return 0

        lax.fori_loop(0, (note_ref[source, BLOCK - 1] + 5) // 6, step, 0)
    if not last:
        return
    over = jnp.min(acts[:, 0, 0:16, 0:BLOCK].astype(f32)) < 0.0
    spoilt = jnp.where(over, jnp.nan, 0.0).astype(f32)

    def write(ref, n, half, p):
        top = half * BLOCK + 32 * p
        for target, c in itertools.product(range(4), range(6)):
            total = acc[target * 6 + c, top : top + 32, :] + before[target * 6 + c, top : top + 32, :] + spoilt
            ref[n, target, :, c * BLOCK : (c + 1) * BLOCK] = total.astype(ref.dtype)

    write(to_near, 0, 0, 1)
    write(to_near, 1, 0, 3)
    write(to_far, 0, 1, 2)
    write(to_far, 1, 1, 3)
    write(keep, 0, 0, 0)
    write(keep, 1, 1, 0)
    write(keep, 2, 0, 2)
    write(keep, 3, 1, 1)


def down(at, packs, hidden, before=None):
    vmem = pl.BlockSpec(memory_space=pltpu.VMEM)
    sums = jax.ShapeDtypeStruct((24, 2 * BLOCK, BLOCK), f32)
    pieces = [jax.ShapeDtypeStruct((2, 4, 32, 6 * BLOCK), bf16)] * 2
    pieces += [jax.ShapeDtypeStruct((4, 4, 32, 6 * BLOCK), f32)]
    last = before is not None
    return pl.pallas_call(
        functools.partial(down_kernel, last),
        out_shape=pieces if last else sums,
        in_specs=[pl.BlockSpec(memory_space=pltpu.SMEM), vmem] + [pl.BlockSpec(memory_space=pl.ANY)] * 5 + [vmem] * last,
        out_specs=[vmem] * 3 if last else vmem,
        scratch_shapes=[pltpu.VMEM((4, 2, 64, 12 * BLOCK), bf16)]
        + [pltpu.VMEM(sums.shape, f32)] * last
        + [pltpu.SemaphoreType.DMA((8,)), *notes(4)],
        compiler_params=pltpu.CompilerParams(vmem_limit_bytes=DOWN_LIMIT),
    )(at, packs, *hidden, *([before] if last else []))


def body(tokens, up_weight, up_mask, up_bias, down_weight, down_mask, down_bias):
    at = jnp.stack([lax.axis_index(axis) for axis in AXES]).astype(jnp.int32)

    z = ("zh", "zl")
    rows = tokens.reshape(4, 1, 32, 6 * BLOCK)
    own = spread(jnp.broadcast_to(rows, (4, 2, 32, 6 * BLOCK)).reshape(8, 32, 6 * BLOCK), z)
    own = own.reshape(4, 2, 32, 6 * BLOCK)
    up_own = pack_up(up_mask, down_mask, up_weight)
    biases = jnp.stack([up_bias, swap_core(up_bias)])
    other_down, other_mask = swap_core(down_weight), swap_core(down_mask)
    own, other_down, other_mask, _ = together(own, other_down, other_mask, up_own)

    up_mine = [up_own] + [send(up_own, flip("zh", mask)) for mask in (1, 3, 2)]
    near, far = ring_first(own, "x")
    down_packed = pack_down(at, down_mask, other_mask, down_mask, other_mask, down_weight, other_down)
    near, far, down_packed = together(near, far, down_packed)
    left, right = ring_second(near, far, "x")
    up_other = [swap_core(pack) for pack in up_mine]
    up_mine, left, right, down_packed, biases = together(up_mine, left, right, down_packed, biases)

    down_mine = spread(down_packed)
    to_near, to_far, keep, flag = up(at, up_mine + up_other, [own, near, far, left, right])

    near, far = sum_first(to_near, to_far, "y")
    near, far = together(near, far)
    last, first = sum_second(near, far, keep, "y")
    sums = jnp.stack(summed(keep, near, far, last, first))
    hidden = jnp.maximum(sums + biases[:, None, :], 0.0).astype(bf16)
    over = flag[0, 0] > 0
    marked = jnp.where(over, -jnp.ones_like(hidden), hidden)
    near, far = ring_first(marked, "y")
    near, far = together(near, far)
    left, right = ring_second(near, far, "y")
    left, right, down_mine = together(left, right, down_mine)

    down_other = swap_core(down_mine)
    hiddens = [marked, near, far, left, right]
    to_near, to_far, keep = down(at, down_other, hiddens, down(at, down_mine, hiddens))

    def place(*sums):
        pieces = jnp.stack(sums, axis=1).astype(bf16).reshape(8, 32, 6 * BLOCK)
        got = spread(pieces, z).reshape(4, 2, 32, 6 * BLOCK).astype(f32)
        return (got[:, 0] + got[:, 1] + down_bias).astype(bf16).reshape(BLOCK, 6 * BLOCK)

    near, far = sum_first(to_near, to_far, "x")
    last, first = sum_second(near, far, keep, "x")
    out = place(*summed(keep, near, far, last, first))

    def whole(_):
        kept = lax.all_gather(expand_mask(down_mask, down_weight), "zh")
        kept = jnp.stack([kept, swap_core(kept)]).transpose(0, 2, 1, 3).reshape(24 * BLOCK, 24 * BLOCK)
        acts = lax.all_gather(hidden, "y").transpose(0, 2, 1, 3).reshape(2 * BLOCK, 24 * BLOCK)
        sums = jnp.dot(acts, kept, preferred_element_type=f32).reshape(2, 4, 32, 4, 6 * BLOCK)
        x = lax.axis_index("x")
        order = jnp.array([0, 1, 3, 2])[x ^ jnp.arange(4)]
        sums = lax.psum(jnp.take(sums, order, axis=1), "x")
        sums = lax.dynamic_index_in_dim(sums, x, 1, keepdims=False).transpose(0, 2, 1, 3)
        return place(sums[0], sums[1])

    return lax.cond(jnp.isnan(out[0, 0]), whole, lambda _: out, 0)


def solution(mesh):
    fine = Mesh(mesh.devices.reshape(SIZES), AXES)
    in_specs = (P(ROW, COL), P(COL, ROW), P(COL, ROW), P(ROW), P(ROW, COL), P(ROW, COL), P(COL))
    return jax.shard_map(body, mesh=fine, in_specs=in_specs, out_specs=P(ROW, COL), check_vma=False)
```

```python
import functools
import itertools

import jax
import jax.numpy as jnp
from jax import lax
from jax.experimental import pallas as pl
from jax.experimental.pallas import tpu as pltpu
from jax.sharding import Mesh
from jax.sharding import PartitionSpec as P

AXES = ("zl", "x", "core", "zh", "y")
SIZES = (2, 4, 2, 4, 4)
ROW = ("zl", "x", "core")
COL = ("zh", "y")
BLOCK = 128
UP_KEPT = 9
PAIR = 18
VMEM_LIMIT = 50 * 1024 * 1024
DOWN_LIMIT = 40 * 1024 * 1024
bf16 = jnp.bfloat16
f32 = jnp.float32


def flat(coords):
    at = 0
    for value, size in zip(coords, SIZES):
        at = at * size + value
    return at


def route(move):
    pairs = []
    for coords in itertools.product(*[range(size) for size in SIZES]):
        named = dict(zip(AXES, coords))
        named.update(move(**named))
        pairs.append((flat(coords), flat([named[axis] for axis in AXES])))
    return pairs


def flip(axis, mask):
    return route(lambda **at: {axis: at[axis] ^ mask})


def send(array, pairs):
    return lax.ppermute(array, AXES, pairs)


def expand_mask(mask, weight):
    rows, cols = mask.shape
    side = weight.shape[0] // rows
    full = jnp.broadcast_to(mask[:, None, :, None], (rows, side, cols, side)).reshape(weight.shape)
    return jnp.where(full > 0, weight, jnp.zeros_like(weight))


def together(*trees):
    return lax.optimization_barrier(trees)


def first_half(array):
    return array[: array.shape[0] // 2]


def last_half(array):
    return array[array.shape[0] // 2 :]


def swap_core(array):
    return send(array, flip("core", 1))


def ring_first(array, axis):
    return send(array, flip(axis, 1)), send(array, flip(axis, 3))


def ring_second(near, far, axis):
    return send(first_half(near), flip(axis, 3)), send(last_half(far), flip(axis, 1))


def sum_first(to_near, to_far, axis):
    return send(to_near, flip(axis, 1)), send(to_far, flip(axis, 3))


def sum_second(near, far, keep, axis):
    last = send((near[1].astype(f32) + keep[2]).astype(bf16), flip(axis, 3))
    first = send((far[1].astype(f32) + keep[3]).astype(bf16), flip(axis, 1))
    return last, first


def summed(keep, near, far, last, first):
    return keep[0] + near[0].astype(f32) + last.astype(f32), keep[1] + far[0].astype(f32) + first.astype(f32)


def write_notes(out, notes, lane, last, kept, down_kept):
    note = jnp.where(lane == BLOCK - 1, kept.astype(f32), notes[...])
    note = jnp.where(lane == BLOCK - 2, down_kept.astype(f32), note).astype(bf16)
    if len(out.shape) == 3:
        out[last] = note
    else:
        for copy in range(4):
            out[copy, last] = note


def kept_in(mask_ref):
    return jnp.sum((mask_ref[...] > 0).astype(f32)).astype(jnp.int32)


def pack_up_kernel(mask_ref, down_mask_ref, w_ref, out, notes, blocks, found, sems):
    lane = lax.broadcasted_iota(jnp.int32, (16, BLOCK), 1)
    notes[...] = jnp.zeros_like(notes)
    found[0] = 0

    def fetch(i, j, b):
        block = w_ref.at[pl.ds(i * BLOCK, BLOCK), pl.ds(j * BLOCK, BLOCK)]
        return pltpu.make_async_copy(block, blocks.at[b], sems.at[b])

    for i, j in itertools.product(range(6), range(12)):

        @pl.when(mask_ref[i, j] > 0)
        def _(i=i, j=j):
            b = found[0]
            found[0] = b + 1
            fetch(i, j, b).start()
            notes[...] = jnp.where(lane == b, float(12 * i + j), notes[...])

    write_notes(out, notes, lane, 8 * UP_KEPT, found[0], kept_in(down_mask_ref))
    for b in range(UP_KEPT):
        fetch(0, 0, b).wait()
        out[8 * b : 8 * b + 8] = blocks[b].reshape(8, 16, BLOCK)


def pack_down_kernel(at_ref, mask_ref, other_mask_ref, mask_v, other_mask_v, w_ref, other_ref, out, notes, found):
    lane = lax.broadcasted_iota(jnp.int32, (16, BLOCK), 1)
    out[...] = jnp.zeros_like(out)
    notes[...] = jnp.zeros_like(notes)
    core = at_ref[2]
    mine, other = kept_in(mask_v), kept_in(other_mask_v)
    found[0] = jnp.where(core == 0, 0, other - PAIR)
    found[1] = jnp.where(core == 0, mine, -PAIR)
    for n, (mask, weight) in enumerate(((mask_ref, w_ref), (other_mask_ref, other_ref))):
        name = 72 * (core ^ n)
        for i, j in itertools.product(range(12), range(6)):

            @pl.when(mask[i, j] > 0)
            def _(i=i, j=j, n=n, name=name, weight=weight):
                b = found[n]
                found[n] = b + 1

                @pl.when((b >= 0) & (b < PAIR))
                def _():
                    notes[...] = jnp.where(lane == b, (name + 6 * i + j).astype(f32), notes[...])
                    block = weight[i * BLOCK : (i + 1) * BLOCK, j * BLOCK : (j + 1) * BLOCK].reshape(8, 16, BLOCK)
                    for copy in range(4):
                        out[copy, pl.ds(8 * b, 8)] = block

    kept = jnp.clip(mine + other - PAIR * core, 0, PAIR)
    write_notes(out, notes, lane, 8 * PAIR, kept, mine)


def pack_up(mask, down_mask, weight):
    vmem = pl.BlockSpec(memory_space=pltpu.VMEM)
    return pl.pallas_call(
        pack_up_kernel,
        out_shape=jax.ShapeDtypeStruct((8 * UP_KEPT + 1, 16, BLOCK), bf16),
        in_specs=[pl.BlockSpec(memory_space=pltpu.SMEM), vmem, pl.BlockSpec(memory_space=pltpu.HBM)],
        out_specs=vmem,
        scratch_shapes=[
            pltpu.VMEM((16, BLOCK), f32),
            pltpu.VMEM((UP_KEPT, BLOCK, BLOCK), bf16),
            pltpu.SMEM((1,), jnp.int32),
            pltpu.SemaphoreType.DMA((UP_KEPT,)),
        ],
        compiler_params=pltpu.CompilerParams(vmem_limit_bytes=VMEM_LIMIT),
    )(mask, down_mask, weight)


def pack_down(*args):
    smem = pl.BlockSpec(memory_space=pltpu.SMEM)
    vmem = pl.BlockSpec(memory_space=pltpu.VMEM)
    return pl.pallas_call(
        pack_down_kernel,
        out_shape=jax.ShapeDtypeStruct((4, 8 * PAIR + 1, 16, BLOCK), bf16),
        in_specs=[smem] * 3 + [vmem] * 4,
        out_specs=vmem,
        scratch_shapes=[pltpu.VMEM((16, BLOCK), f32), pltpu.SMEM((2,), jnp.int32)],
        compiler_params=pltpu.CompilerParams(vmem_limit_bytes=VMEM_LIMIT),
    )(*args)


def spread(array, axis="zh"):
    return lax.all_to_all(array, axis, split_axis=0, concat_axis=0, tiled=True)


def read_notes(rows, staged, note_ref, sem):
    for n, row in enumerate(rows):
        staged[n : n + 1] = row.astype(f32).astype(jnp.int32)
    copy = pltpu.make_async_copy(staged, note_ref, sem)
    copy.start()
    copy.wait()


def notes(rows):
    return [pltpu.VMEM((rows, BLOCK), jnp.int32), pltpu.SMEM((rows, BLOCK), jnp.int32), pltpu.SemaphoreType.DMA]


def up_kernel(at_ref, note_ref, *refs):
    weights, tokens, (to_near, to_far, keep) = (refs[:4], refs[4:8]), refs[8:13], refs[13:16]
    acts, acc0, acc1, sems = refs[16:]
    zh, y = at_ref[3], at_ref[4]
    copies = []
    for p, s, source in itertools.product(range(4), range(2), range(4)):
        part = tokens[p].at[source, s] if p < 3 else tokens[3 + source // 2].at[source % 2, s]
        copies.append(pltpu.make_async_copy(part, acts.at[source, s, p], sems.at[8 * p + 4 * s + source]))
    for copy in copies:
        copy.start()
    accs = (acc0, acc1)
    for acc in accs:
        acc[...] = jnp.zeros_like(acc)
    for copy in copies:
        copy.wait()
    for p, mask in enumerate((0, 1, 3, 2)):
        sums = []
        for b, side in itertools.product(range(UP_KEPT), range(2)):
            cell = note_ref[side, p, b]
            i, c = cell // 12, cell % 12
            left = pl.multiple_of(i * BLOCK, BLOCK)
            block = weights[side][p][8 * b : 8 * b + 8].reshape(BLOCK, BLOCK)
            some = acts[zh ^ mask, :, :, :, pl.ds(left, BLOCK)].reshape(2 * BLOCK, BLOCK)
            sums.append((side, c, jnp.dot(some, block, preferred_element_type=f32)))
        for side, c, more in sums:
            accs[side][c] += more

    def write(ref, n, side, mask):
        top = pl.multiple_of((y ^ mask) * 64, 64)
        for c in range(12):
            ref[n, :, c * BLOCK : (c + 1) * BLOCK] = accs[side][c, pl.ds(top, 64), :].astype(ref.dtype)

    write(to_near, 0, 0, 1)
    write(to_near, 1, 0, 2)
    write(to_far, 0, 1, 3)
    write(to_far, 1, 1, 2)
    write(keep, 0, 0, 0)
    write(keep, 1, 1, 0)
    write(keep, 2, 0, 3)
    write(keep, 3, 1, 1)


def up(at, notes, weights, tokens):
    smem = pl.BlockSpec(memory_space=pltpu.SMEM)
    vmem = pl.BlockSpec(memory_space=pltpu.VMEM)
    hbm = pl.BlockSpec(memory_space=pl.ANY)
    return pl.pallas_call(
        up_kernel,
        out_shape=[
            jax.ShapeDtypeStruct((2, 64, 12 * BLOCK), bf16),
            jax.ShapeDtypeStruct((2, 64, 12 * BLOCK), bf16),
            jax.ShapeDtypeStruct((4, 64, 12 * BLOCK), f32),
        ],
        in_specs=[smem, smem] + [vmem] * 8 + [hbm] * 5,
        out_specs=[vmem] * 3,
        scratch_shapes=[
            pltpu.VMEM((4, 2, 4, 32, 6 * BLOCK), bf16),
            pltpu.VMEM((12, 2 * BLOCK, BLOCK), f32),
            pltpu.VMEM((12, 2 * BLOCK, BLOCK), f32),
            pltpu.SemaphoreType.DMA((32,)),
        ],
        compiler_params=pltpu.CompilerParams(vmem_limit_bytes=VMEM_LIMIT),
    )(at, notes, *weights, *tokens)


def down_kernel(last, at_ref, *refs):
    packs, hidden = refs[0], refs[1:6]
    if last:
        before, to_near, to_far, keep = refs[6:10]
        acts, acc, sems, staged, note_ref, note_sem = refs[10:]
    else:
        acc = refs[6]
        acts, sems, staged, note_ref, note_sem = refs[7:]
    core, y = at_ref[2], at_ref[4]
    copies = []
    for n, mask in enumerate((0, 1, 3, 2)):
        for side in range(2):
            part = hidden[n].at[side] if mask != 2 else hidden[3 + side].at[0]
            copies.append(pltpu.make_async_copy(part, acts.at[y ^ mask, side], sems.at[2 * n + side]))
    for copy in copies:
        copy.start()
    read_notes([packs[source, 8 * PAIR, 0:1] for source in range(4)], staged, note_ref, note_sem)
    acc[...] = jnp.zeros_like(acc)
    for copy in copies:
        copy.wait()
    for source in range(4):

        def step(group, _, source=source):
            sums = []
            for n in range(6):
                b = 6 * group + n
                name = note_ref[source, b]
                of = (name >= 72).astype(jnp.int32)
                cell = name - 72 * of
                i, c = cell // 6, cell % 6
                left = pl.multiple_of(i * BLOCK, BLOCK)
                block = packs[source, pl.ds(8 * b, 8)].reshape(BLOCK, BLOCK)
                some = acts[:, of ^ core, :, pl.ds(left, BLOCK)].reshape(2 * BLOCK, BLOCK)
                sums.append((source * 6 + c, jnp.dot(some, block, preferred_element_type=f32)))
            for c, more in sums:
                acc[c] += more
            return 0

        lax.fori_loop(0, (note_ref[source, BLOCK - 1] + 5) // 6, step, 0)
    if not last:
        return
    over = jnp.min(acts[:, 0, 0:16, 0:BLOCK].astype(f32)) < 0.0
    spoilt = jnp.where(over, jnp.nan, 0.0).astype(f32)

    def write(ref, n, half, p):
        top = half * BLOCK + 32 * p
        for target, c in itertools.product(range(4), range(6)):
            total = acc[target * 6 + c, top : top + 32, :] + before[target * 6 + c, top : top + 32, :] + spoilt
            ref[n, target, :, c * BLOCK : (c + 1) * BLOCK] = total.astype(ref.dtype)

    write(to_near, 0, 0, 1)
    write(to_near, 1, 0, 3)
    write(to_far, 0, 1, 2)
    write(to_far, 1, 1, 3)
    write(keep, 0, 0, 0)
    write(keep, 1, 1, 0)
    write(keep, 2, 0, 2)
    write(keep, 3, 1, 1)


def down(at, packs, hidden, before=None):
    vmem = pl.BlockSpec(memory_space=pltpu.VMEM)
    sums = jax.ShapeDtypeStruct((24, 2 * BLOCK, BLOCK), f32)
    pieces = [jax.ShapeDtypeStruct((2, 4, 32, 6 * BLOCK), bf16)] * 2
    pieces += [jax.ShapeDtypeStruct((4, 4, 32, 6 * BLOCK), f32)]
    last = before is not None
    return pl.pallas_call(
        functools.partial(down_kernel, last),
        out_shape=pieces if last else sums,
        in_specs=[pl.BlockSpec(memory_space=pltpu.SMEM), vmem] + [pl.BlockSpec(memory_space=pl.ANY)] * 5 + [vmem] * last,
        out_specs=[vmem] * 3 if last else vmem,
        scratch_shapes=[pltpu.VMEM((4, 2, 64, 12 * BLOCK), bf16)]
        + [pltpu.VMEM(sums.shape, f32)] * last
        + [pltpu.SemaphoreType.DMA((8,)), *notes(4)],
        compiler_params=pltpu.CompilerParams(vmem_limit_bytes=DOWN_LIMIT),
    )(at, packs, *hidden, *([before] if last else []))


def body(tokens, up_weight, up_mask, up_bias, down_weight, down_mask, down_bias):
    at = jnp.stack([lax.axis_index(axis) for axis in AXES]).astype(jnp.int32)

    z = ("zh", "zl")
    rows = tokens.reshape(4, 1, 32, 6 * BLOCK)
    own = spread(jnp.broadcast_to(rows, (4, 2, 32, 6 * BLOCK)).reshape(8, 32, 6 * BLOCK), z)
    own = own.reshape(4, 2, 32, 6 * BLOCK)
    up_own = pack_up(up_mask, down_mask, up_weight)
    biases = jnp.stack([up_bias, swap_core(up_bias)])
    other_down, other_mask = swap_core(down_weight), swap_core(down_mask)

    up_mine = [up_own] + [send(up_own, flip("zh", mask)) for mask in (1, 3, 2)]
    near, far = ring_first(own, "x")
    down_packed = pack_down(at, down_mask, other_mask, down_mask, other_mask, down_weight, other_down)
    near, far, down_packed = together(near, far, down_packed)
    left, right = ring_second(near, far, "x")
    up_other = [swap_core(pack) for pack in up_mine]
    up_mine, left, right, down_packed, biases = together(up_mine, left, right, down_packed, biases)

    down_mine = spread(down_packed)
    up_packs = up_mine + up_other
    up_notes = jnp.stack([pack[8 * UP_KEPT, 0] for pack in up_packs]).astype(jnp.int32).reshape(2, 4, BLOCK)
    to_near, to_far, keep = up(at, up_notes, up_packs, [own, near, far, left, right])

    near, far = sum_first(to_near, to_far, "y")
    near, far = together(near, far)
    last, first = sum_second(near, far, keep, "y")
    sums = jnp.stack(summed(keep, near, far, last, first))
    hidden = jnp.maximum(sums + biases[:, None, :], 0.0).astype(bf16)
    over = jnp.max(up_notes[0, :, BLOCK - 2] + up_notes[1, :, BLOCK - 2]) > 2 * PAIR
    marked = jnp.where(over, -jnp.ones_like(hidden), hidden)
    near, far = ring_first(marked, "y")
    near, far = together(near, far)
    left, right = ring_second(near, far, "y")
    left, right, down_mine = together(left, right, down_mine)

    down_other = swap_core(down_mine)
    hiddens = [marked, near, far, left, right]
    to_near, to_far, keep = down(at, down_other, hiddens, down(at, down_mine, hiddens))

    def place(*sums):
        pieces = jnp.stack(sums, axis=1).astype(bf16).reshape(8, 32, 6 * BLOCK)
        got = spread(pieces, z).reshape(4, 2, 32, 6 * BLOCK).astype(f32)
        return (got[:, 0] + got[:, 1] + down_bias).astype(bf16).reshape(BLOCK, 6 * BLOCK)

    near, far = sum_first(to_near, to_far, "x")
    last, first = sum_second(near, far, keep, "x")
    out = place(*summed(keep, near, far, last, first))

    def whole(_):
        kept = lax.all_gather(expand_mask(down_mask, down_weight), "zh")
        kept = jnp.stack([kept, swap_core(kept)]).transpose(0, 2, 1, 3).reshape(24 * BLOCK, 24 * BLOCK)
        acts = lax.all_gather(hidden, "y").transpose(0, 2, 1, 3).reshape(2 * BLOCK, 24 * BLOCK)
        sums = jnp.dot(acts, kept, preferred_element_type=f32).reshape(2, 4, 32, 4, 6 * BLOCK)
        x = lax.axis_index("x")
        order = jnp.array([0, 1, 3, 2])[x ^ jnp.arange(4)]
        sums = lax.psum(jnp.take(sums, order, axis=1), "x")
        sums = lax.dynamic_index_in_dim(sums, x, 1, keepdims=False).transpose(0, 2, 1, 3)
        return place(sums[0], sums[1])

    return lax.cond(jnp.isnan(out[0, 0]), whole, lambda _: out, 0)


def solution(mesh):
    fine = Mesh(mesh.devices.reshape(SIZES), AXES)
    in_specs = (P(ROW, COL), P(COL, ROW), P(COL, ROW), P(ROW), P(ROW, COL), P(ROW, COL), P(COL))
    return jax.shard_map(body, mesh=fine, in_specs=in_specs, out_specs=P(ROW, COL), check_vma=False)
```

```python
import functools
import itertools

import jax
import jax.numpy as jnp
from jax import lax
from jax.experimental import pallas as pl
from jax.experimental.pallas import tpu as pltpu
from jax.sharding import Mesh
from jax.sharding import PartitionSpec as P

AXES = ("zl", "x", "core", "zh", "y")
SIZES = (2, 4, 2, 4, 4)
ROW = ("zl", "x", "core")
COL = ("zh", "y")
BLOCK = 128
UP_KEPT = 9
PAIR = 18
VMEM_LIMIT = 50 * 1024 * 1024
DOWN_LIMIT = 40 * 1024 * 1024
bf16 = jnp.bfloat16
f32 = jnp.float32


def flat(coords):
    at = 0
    for value, size in zip(coords, SIZES):
        at = at * size + value
    return at


def route(move):
    pairs = []
    for coords in itertools.product(*[range(size) for size in SIZES]):
        named = dict(zip(AXES, coords))
        named.update(move(**named))
        pairs.append((flat(coords), flat([named[axis] for axis in AXES])))
    return pairs


def flip(axis, mask):
    return route(lambda **at: {axis: at[axis] ^ mask})


def send(array, pairs):
    return lax.ppermute(array, AXES, pairs)


def expand_mask(mask, weight):
    rows, cols = mask.shape
    side = weight.shape[0] // rows
    full = jnp.broadcast_to(mask[:, None, :, None], (rows, side, cols, side)).reshape(weight.shape)
    return jnp.where(full > 0, weight, jnp.zeros_like(weight))


def together(*trees):
    return lax.optimization_barrier(trees)


def first_half(array):
    return array[: array.shape[0] // 2]


def last_half(array):
    return array[array.shape[0] // 2 :]


def swap_core(array):
    return send(array, flip("core", 1))


def ring_first(array, axis):
    return send(array, flip(axis, 1)), send(array, flip(axis, 3))


def ring_second(near, far, axis):
    return send(first_half(near), flip(axis, 3)), send(last_half(far), flip(axis, 1))


def sum_first(to_near, to_far, axis):
    return send(to_near, flip(axis, 1)), send(to_far, flip(axis, 3))


def sum_second(near, far, keep, axis):
    last = send((near[1].astype(f32) + keep[2]).astype(bf16), flip(axis, 3))
    first = send((far[1].astype(f32) + keep[3]).astype(bf16), flip(axis, 1))
    return last, first


def summed(keep, near, far, last, first):
    return keep[0] + near[0].astype(f32) + last.astype(f32), keep[1] + far[0].astype(f32) + first.astype(f32)


def write_notes(out, notes, lane, last, kept, down_kept):
    note = jnp.where(lane == BLOCK - 1, kept.astype(f32), notes[...])
    note = jnp.where(lane == BLOCK - 2, down_kept.astype(f32), note).astype(bf16)
    for copy in range(4):
        out[copy, last] = note


def kept_in(mask_ref):
    return jnp.sum((mask_ref[...] > 0).astype(f32)).astype(jnp.int32)


def pack_up_kernel(mask_ref, down_mask_ref, w_ref, out, notes, found):
    lane = lax.broadcasted_iota(jnp.int32, (16, BLOCK), 1)
    notes[...] = jnp.zeros_like(notes)
    found[0] = 0
    for i, j in itertools.product(range(6), range(12)):

        @pl.when(mask_ref[i, j] > 0)
        def _(i=i, j=j):
            b = found[0]
            found[0] = b + 1
            notes[...] = jnp.where(lane == b, float(12 * i + j), notes[...])
            block = w_ref[i * BLOCK : (i + 1) * BLOCK, j * BLOCK : (j + 1) * BLOCK].reshape(8, 16, BLOCK)
            for copy in range(4):
                out[copy, pl.ds(8 * b, 8)] = block

    write_notes(out, notes, lane, 8 * UP_KEPT, found[0], kept_in(down_mask_ref))


def pack_down_kernel(at_ref, mask_ref, other_mask_ref, mask_v, other_mask_v, w_ref, other_ref, out, notes, found):
    lane = lax.broadcasted_iota(jnp.int32, (16, BLOCK), 1)
    out[...] = jnp.zeros_like(out)
    notes[...] = jnp.zeros_like(notes)
    core = at_ref[2]
    mine, other = kept_in(mask_v), kept_in(other_mask_v)
    found[0] = jnp.where(core == 0, 0, other - PAIR)
    found[1] = jnp.where(core == 0, mine, -PAIR)
    for n, (mask, weight) in enumerate(((mask_ref, w_ref), (other_mask_ref, other_ref))):
        name = 72 * (core ^ n)
        for i, j in itertools.product(range(12), range(6)):

            @pl.when(mask[i, j] > 0)
            def _(i=i, j=j, n=n, name=name, weight=weight):
                b = found[n]
                found[n] = b + 1

                @pl.when((b >= 0) & (b < PAIR))
                def _():
                    notes[...] = jnp.where(lane == b, (name + 6 * i + j).astype(f32), notes[...])
                    block = weight[i * BLOCK : (i + 1) * BLOCK, j * BLOCK : (j + 1) * BLOCK].reshape(8, 16, BLOCK)
                    for copy in range(4):
                        out[copy, pl.ds(8 * b, 8)] = block

    kept = jnp.clip(mine + other - PAIR * core, 0, PAIR)
    write_notes(out, notes, lane, 8 * PAIR, kept, mine)


def pack(kernel, cap, *args):
    smem = pl.BlockSpec(memory_space=pltpu.SMEM)
    vmem = pl.BlockSpec(memory_space=pltpu.VMEM)
    return pl.pallas_call(
        kernel,
        out_shape=jax.ShapeDtypeStruct((4, 8 * cap + 1, 16, BLOCK), bf16),
        in_specs=[smem, vmem, vmem] if kernel is pack_up_kernel else [smem] * 3 + [vmem] * 4,
        out_specs=vmem,
        scratch_shapes=[pltpu.VMEM((16, BLOCK), f32), pltpu.SMEM((2,), jnp.int32)],
        compiler_params=pltpu.CompilerParams(vmem_limit_bytes=VMEM_LIMIT),
    )(*args)


def spread(array, axis="zh"):
    return lax.all_to_all(array, axis, split_axis=0, concat_axis=0, tiled=True)


def notes_of(mine, other, cap):
    return jnp.stack([mine[:, 8 * cap, 0], other[:, 8 * cap, 0]]).astype(jnp.int32)


def up_kernel(at_ref, note_ref, *refs):
    weights, tokens, (to_near, to_far, keep) = refs[:2], refs[2:7], refs[7:10]
    acts, acc0, acc1, sems = refs[10:]
    y = at_ref[4]
    copies = []
    for p, s, source in itertools.product(range(4), range(2), range(4)):
        part = tokens[p].at[source, s] if p < 3 else tokens[3 + source // 2].at[source % 2, s]
        copies.append(pltpu.make_async_copy(part, acts.at[source, s, p], sems.at[8 * p + 4 * s + source]))
    for copy in copies:
        copy.start()
    accs = (acc0, acc1)
    for acc in accs:
        acc[...] = jnp.zeros_like(acc)
    for copy in copies:
        copy.wait()
    for source in range(4):

        def step(group, _):
            sums = []
            for n, side in itertools.product(range(3), range(2)):
                b = 3 * group + n
                cell = note_ref[side, source, b]
                i, c = cell // 12, cell % 12
                left = pl.multiple_of(i * BLOCK, BLOCK)
                block = weights[side][source, pl.ds(8 * b, 8)].reshape(BLOCK, BLOCK)
                some = acts[source, :, :, :, pl.ds(left, BLOCK)].reshape(2 * BLOCK, BLOCK)
                sums.append((side, c, jnp.dot(some, block, preferred_element_type=f32)))
            for side, c, more in sums:
                accs[side][c] += more
            return 0

        lax.fori_loop(0, UP_KEPT // 3, step, 0)

    def write(ref, n, side, mask):
        top = pl.multiple_of((y ^ mask) * 64, 64)
        for c in range(12):
            ref[n, :, c * BLOCK : (c + 1) * BLOCK] = accs[side][c, pl.ds(top, 64), :].astype(ref.dtype)

    write(to_near, 0, 0, 1)
    write(to_near, 1, 0, 2)
    write(to_far, 0, 1, 3)
    write(to_far, 1, 1, 2)
    write(keep, 0, 0, 0)
    write(keep, 1, 1, 0)
    write(keep, 2, 0, 3)
    write(keep, 3, 1, 1)


def up(at, notes, weights, tokens):
    smem = pl.BlockSpec(memory_space=pltpu.SMEM)
    vmem = pl.BlockSpec(memory_space=pltpu.VMEM)
    hbm = pl.BlockSpec(memory_space=pl.ANY)
    return pl.pallas_call(
        up_kernel,
        out_shape=[
            jax.ShapeDtypeStruct((2, 64, 12 * BLOCK), bf16),
            jax.ShapeDtypeStruct((2, 64, 12 * BLOCK), bf16),
            jax.ShapeDtypeStruct((4, 64, 12 * BLOCK), f32),
        ],
        in_specs=[smem, smem, vmem, vmem] + [hbm] * 5,
        out_specs=[vmem] * 3,
        scratch_shapes=[
            pltpu.VMEM((4, 2, 4, 32, 6 * BLOCK), bf16),
            pltpu.VMEM((12, 2 * BLOCK, BLOCK), f32),
            pltpu.VMEM((12, 2 * BLOCK, BLOCK), f32),
            pltpu.SemaphoreType.DMA((32,)),
        ],
        compiler_params=pltpu.CompilerParams(vmem_limit_bytes=VMEM_LIMIT),
    )(at, notes, *weights, *tokens)


def down_kernel(last, at_ref, note_ref, *refs):
    packs, hidden = refs[0], refs[1:6]
    if last:
        before, to_near, to_far, keep = refs[6:10]
        acts, acc, sems = refs[10:]
    else:
        acc = refs[6]
        acts, sems = refs[7:]
    core, y = at_ref[2], at_ref[4]
    copies = []
    for n, mask in enumerate((0, 1, 3, 2)):
        for side in range(2):
            part = hidden[n].at[side] if mask != 2 else hidden[3 + side].at[0]
            copies.append(pltpu.make_async_copy(part, acts.at[y ^ mask, side], sems.at[2 * n + side]))
    for copy in copies:
        copy.start()
    acc[...] = jnp.zeros_like(acc)
    for copy in copies:
        copy.wait()
    for source in range(4):

        def step(group, _, source=source):
            sums = []
            for n in range(6):
                b = 6 * group + n
                name = note_ref[source, b]
                of = (name >= 72).astype(jnp.int32)
                cell = name - 72 * of
                i, c = cell // 6, cell % 6
                left = pl.multiple_of(i * BLOCK, BLOCK)
                block = packs[source, pl.ds(8 * b, 8)].reshape(BLOCK, BLOCK)
                some = acts[:, of ^ core, :, pl.ds(left, BLOCK)].reshape(2 * BLOCK, BLOCK)
                sums.append((source * 6 + c, jnp.dot(some, block, preferred_element_type=f32)))
            for c, more in sums:
                acc[c] += more
            return 0

        lax.fori_loop(0, (note_ref[source, BLOCK - 1] + 5) // 6, step, 0)
    if not last:
        return
    over = jnp.min(acts[:, 0, 0:16, 0:BLOCK].astype(f32)) < 0.0
    spoilt = jnp.where(over, jnp.nan, 0.0).astype(f32)

    def write(ref, n, half, p):
        top = half * BLOCK + 32 * p
        for target, c in itertools.product(range(4), range(6)):
            total = acc[target * 6 + c, top : top + 32, :] + before[target * 6 + c, top : top + 32, :] + spoilt
            ref[n, target, :, c * BLOCK : (c + 1) * BLOCK] = total.astype(ref.dtype)

    write(to_near, 0, 0, 1)
    write(to_near, 1, 0, 3)
    write(to_far, 0, 1, 2)
    write(to_far, 1, 1, 3)
    write(keep, 0, 0, 0)
    write(keep, 1, 1, 0)
    write(keep, 2, 0, 2)
    write(keep, 3, 1, 1)


def down(at, packs, hidden, before=None):
    smem = pl.BlockSpec(memory_space=pltpu.SMEM)
    places = packs[:, 8 * PAIR, 0].astype(jnp.int32)
    vmem = pl.BlockSpec(memory_space=pltpu.VMEM)
    sums = jax.ShapeDtypeStruct((24, 2 * BLOCK, BLOCK), f32)
    pieces = [jax.ShapeDtypeStruct((2, 4, 32, 6 * BLOCK), bf16)] * 2
    pieces += [jax.ShapeDtypeStruct((4, 4, 32, 6 * BLOCK), f32)]
    last = before is not None
    return pl.pallas_call(
        functools.partial(down_kernel, last),
        out_shape=pieces if last else sums,
        in_specs=[smem, smem, vmem] + [pl.BlockSpec(memory_space=pl.ANY)] * 5 + [vmem] * last,
        out_specs=[vmem] * 3 if last else vmem,
        scratch_shapes=[pltpu.VMEM((4, 2, 64, 12 * BLOCK), bf16)]
        + [pltpu.VMEM(sums.shape, f32)] * last
        + [pltpu.SemaphoreType.DMA((8,))],
        compiler_params=pltpu.CompilerParams(vmem_limit_bytes=DOWN_LIMIT),
    )(at, places, packs, *hidden, *([before] if last else []))


def body(tokens, up_weight, up_mask, up_bias, down_weight, down_mask, down_bias):
    at = jnp.stack([lax.axis_index(axis) for axis in AXES]).astype(jnp.int32)

    z = ("zh", "zl")
    rows = tokens.reshape(4, 1, 32, 6 * BLOCK)
    own = spread(jnp.broadcast_to(rows, (4, 2, 32, 6 * BLOCK)).reshape(8, 32, 6 * BLOCK), z)
    own = own.reshape(4, 2, 32, 6 * BLOCK)
    up_packed = pack(pack_up_kernel, UP_KEPT, up_mask, down_mask, up_weight)
    biases = jnp.stack([up_bias, swap_core(up_bias)])
    other_down, other_mask = swap_core(down_weight), swap_core(down_mask)

    up_mine = spread(up_packed)
    near, far = ring_first(own, "x")
    down_packed = pack(
        pack_down_kernel, PAIR, at, down_mask, other_mask, down_mask, other_mask, down_weight, other_down
    )
    near, far, down_packed = together(near, far, down_packed)
    left, right = ring_second(near, far, "x")
    up_mine, left, right, down_packed, biases = together(up_mine, left, right, down_packed, biases)

    up_other = swap_core(up_mine)
    down_mine = spread(down_packed)
    up_notes = notes_of(up_mine, up_other, UP_KEPT)
    to_near, to_far, keep = up(at, up_notes, [up_mine, up_other], [own, near, far, left, right])

    near, far = sum_first(to_near, to_far, "y")
    near, far = together(near, far)
    last, first = sum_second(near, far, keep, "y")
    sums = jnp.stack(summed(keep, near, far, last, first))
    hidden = jnp.maximum(sums + biases[:, None, :], 0.0).astype(bf16)
    over = jnp.max(up_notes[0, :, BLOCK - 2] + up_notes[1, :, BLOCK - 2]) > 2 * PAIR
    marked = jnp.where(over, -jnp.ones_like(hidden), hidden)
    near, far = ring_first(marked, "y")
    near, far = together(near, far)
    left, right = ring_second(near, far, "y")
    left, right, down_mine = together(left, right, down_mine)

    down_other = swap_core(down_mine)
    hiddens = [marked, near, far, left, right]
    to_near, to_far, keep = down(at, down_other, hiddens, down(at, down_mine, hiddens))

    def place(*sums):
        pieces = jnp.stack(sums, axis=1).astype(bf16).reshape(8, 32, 6 * BLOCK)
        got = spread(pieces, z).reshape(4, 2, 32, 6 * BLOCK).astype(f32)
        return (got[:, 0] + got[:, 1] + down_bias).astype(bf16).reshape(BLOCK, 6 * BLOCK)

    near, far = sum_first(to_near, to_far, "x")
    last, first = sum_second(near, far, keep, "x")
    out = place(*summed(keep, near, far, last, first))

    def whole(_):
        kept = lax.all_gather(expand_mask(down_mask, down_weight), "zh")
        kept = jnp.stack([kept, swap_core(kept)]).transpose(0, 2, 1, 3).reshape(24 * BLOCK, 24 * BLOCK)
        acts = lax.all_gather(hidden, "y").transpose(0, 2, 1, 3).reshape(2 * BLOCK, 24 * BLOCK)
        sums = jnp.dot(acts, kept, preferred_element_type=f32).reshape(2, 4, 32, 4, 6 * BLOCK)
        x = lax.axis_index("x")
        order = jnp.array([0, 1, 3, 2])[x ^ jnp.arange(4)]
        sums = lax.psum(jnp.take(sums, order, axis=1), "x")
        sums = lax.dynamic_index_in_dim(sums, x, 1, keepdims=False).transpose(0, 2, 1, 3)
        return place(sums[0], sums[1])

    return lax.cond(jnp.isnan(out[0, 0]), whole, lambda _: out, 0)


def solution(mesh):
    fine = Mesh(mesh.devices.reshape(SIZES), AXES)
    in_specs = (P(ROW, COL), P(COL, ROW), P(COL, ROW), P(ROW), P(ROW, COL), P(ROW, COL), P(COL))
    return jax.shard_map(body, mesh=fine, in_specs=in_specs, out_specs=P(ROW, COL), check_vma=False)
```

```python
import functools
import itertools

import jax
import jax.numpy as jnp
from jax import lax
from jax.experimental import pallas as pl
from jax.experimental.pallas import tpu as pltpu
from jax.sharding import Mesh
from jax.sharding import PartitionSpec as P

AXES = ("zl", "x", "core", "zh", "y")
SIZES = (2, 4, 2, 4, 4)
ROW = ("zl", "x", "core")
COL = ("zh", "y")
BLOCK = 128
UP_KEPT = 9
PAIR = 18
VMEM_LIMIT = 50 * 1024 * 1024
bf16 = jnp.bfloat16
f32 = jnp.float32


def flat(coords):
    at = 0
    for value, size in zip(coords, SIZES):
        at = at * size + value
    return at


def route(move):
    pairs = []
    for coords in itertools.product(*[range(size) for size in SIZES]):
        named = dict(zip(AXES, coords))
        named.update(move(**named))
        pairs.append((flat(coords), flat([named[axis] for axis in AXES])))
    return pairs


def flip(axis, mask):
    return route(lambda **at: {axis: at[axis] ^ mask})


def send(array, pairs):
    return lax.ppermute(array, AXES, pairs)


def expand_mask(mask, weight):
    rows, cols = mask.shape
    side = weight.shape[0] // rows
    full = jnp.broadcast_to(mask[:, None, :, None], (rows, side, cols, side)).reshape(weight.shape)
    return jnp.where(full > 0, weight, jnp.zeros_like(weight))


def together(*trees):
    return lax.optimization_barrier(trees)


def first_half(array):
    return array[: array.shape[0] // 2]


def last_half(array):
    return array[array.shape[0] // 2 :]


def swap_core(array):
    return send(array, flip("core", 1))


def ring_first(array, axis):
    return send(array, flip(axis, 1)), send(array, flip(axis, 3))


def ring_second(near, far, axis):
    return send(first_half(near), flip(axis, 3)), send(last_half(far), flip(axis, 1))


def sum_first(to_near, to_far, axis):
    return send(to_near, flip(axis, 1)), send(to_far, flip(axis, 3))


def sum_second(near, far, keep, axis):
    last = send((near[1].astype(f32) + keep[2]).astype(bf16), flip(axis, 3))
    first = send((far[1].astype(f32) + keep[3]).astype(bf16), flip(axis, 1))
    return last, first


def summed(keep, near, far, last, first):
    return keep[0] + near[0].astype(f32) + last.astype(f32), keep[1] + far[0].astype(f32) + first.astype(f32)


def write_notes(out, notes, lane, last, kept, down_kept):
    note = jnp.where(lane == BLOCK - 1, kept.astype(f32), notes[...])
    note = jnp.where(lane == BLOCK - 2, down_kept.astype(f32), note).astype(bf16)
    if len(out.shape) == 3:
        out[last] = note
    else:
        for copy in range(4):
            out[copy, last] = note


def kept_in(mask_ref):
    return jnp.sum((mask_ref[...] > 0).astype(f32)).astype(jnp.int32)


def pack_up_kernel(mask_ref, down_mask_ref, w_ref, out, notes, blocks, found, sems):
    lane = lax.broadcasted_iota(jnp.int32, (16, BLOCK), 1)
    notes[...] = jnp.zeros_like(notes)
    found[0] = 0

    def fetch(i, j, b):
        block = w_ref.at[pl.ds(i * BLOCK, BLOCK), pl.ds(j * BLOCK, BLOCK)]
        return pltpu.make_async_copy(block, blocks.at[b], sems.at[b])

    for i, j in itertools.product(range(6), range(12)):

        @pl.when(mask_ref[i, j] > 0)
        def _(i=i, j=j):
            b = found[0]
            found[0] = b + 1
            fetch(i, j, b).start()
            notes[...] = jnp.where(lane == b, float(12 * i + j), notes[...])

    write_notes(out, notes, lane, 8 * UP_KEPT, found[0], kept_in(down_mask_ref))
    for b in range(UP_KEPT):
        fetch(0, 0, b).wait()
        out[8 * b : 8 * b + 8] = blocks[b].reshape(8, 16, BLOCK)


def pack_down_kernel(at_ref, mask_ref, other_mask_ref, mask_v, other_mask_v, w_ref, other_ref, out, notes, found):
    lane = lax.broadcasted_iota(jnp.int32, (16, BLOCK), 1)
    out[...] = jnp.zeros_like(out)
    notes[...] = jnp.zeros_like(notes)
    core = at_ref[2]
    mine, other = kept_in(mask_v), kept_in(other_mask_v)
    found[0] = jnp.where(core == 0, 0, other - PAIR)
    found[1] = jnp.where(core == 0, mine, -PAIR)
    for n, (mask, weight) in enumerate(((mask_ref, w_ref), (other_mask_ref, other_ref))):
        name = 72 * (core ^ n)
        for i, j in itertools.product(range(12), range(6)):

            @pl.when(mask[i, j] > 0)
            def _(i=i, j=j, n=n, name=name, weight=weight):
                b = found[n]
                found[n] = b + 1

                @pl.when((b >= 0) & (b < PAIR))
                def _():
                    notes[...] = jnp.where(lane == b, (name + 6 * i + j).astype(f32), notes[...])
                    block = weight[i * BLOCK : (i + 1) * BLOCK, j * BLOCK : (j + 1) * BLOCK].reshape(8, 16, BLOCK)
                    for copy in range(4):
                        out[copy, pl.ds(8 * b, 8)] = block

    kept = jnp.clip(mine + other - PAIR * core, 0, PAIR)
    write_notes(out, notes, lane, 8 * PAIR, kept, mine)


def pack_up(mask, down_mask, weight):
    vmem = pl.BlockSpec(memory_space=pltpu.VMEM)
    return pl.pallas_call(
        pack_up_kernel,
        out_shape=jax.ShapeDtypeStruct((8 * UP_KEPT + 1, 16, BLOCK), bf16),
        in_specs=[pl.BlockSpec(memory_space=pltpu.SMEM), vmem, pl.BlockSpec(memory_space=pltpu.HBM)],
        out_specs=vmem,
        scratch_shapes=[
            pltpu.VMEM((16, BLOCK), f32),
            pltpu.VMEM((UP_KEPT, BLOCK, BLOCK), bf16),
            pltpu.SMEM((1,), jnp.int32),
            pltpu.SemaphoreType.DMA((UP_KEPT,)),
        ],
        compiler_params=pltpu.CompilerParams(vmem_limit_bytes=VMEM_LIMIT),
    )(mask, down_mask, weight)


def pack_down(*args):
    smem = pl.BlockSpec(memory_space=pltpu.SMEM)
    vmem = pl.BlockSpec(memory_space=pltpu.VMEM)
    return pl.pallas_call(
        pack_down_kernel,
        out_shape=jax.ShapeDtypeStruct((4, 8 * PAIR + 1, 16, BLOCK), bf16),
        in_specs=[smem] * 3 + [vmem] * 4,
        out_specs=vmem,
        scratch_shapes=[pltpu.VMEM((16, BLOCK), f32), pltpu.SMEM((2,), jnp.int32)],
        compiler_params=pltpu.CompilerParams(vmem_limit_bytes=VMEM_LIMIT),
    )(*args)


def spread(array, axis="zh"):
    return lax.all_to_all(array, axis, split_axis=0, concat_axis=0, tiled=True)


def notes_of(mine, other, cap):
    return jnp.stack([mine[:, 8 * cap, 0], other[:, 8 * cap, 0]]).astype(jnp.int32)


def up_kernel(at_ref, note_ref, *refs):
    weights, tokens, (to_near, to_far, keep) = (refs[:4], refs[4:8]), refs[8:13], refs[13:16]
    acts, acc0, acc1, sems = refs[16:]
    zh, y = at_ref[3], at_ref[4]
    copies = []
    for p, s, source in itertools.product(range(4), range(2), range(4)):
        part = tokens[p].at[source, s] if p < 3 else tokens[3 + source // 2].at[source % 2, s]
        copies.append(pltpu.make_async_copy(part, acts.at[source, s, p], sems.at[8 * p + 4 * s + source]))
    for copy in copies:
        copy.start()
    accs = (acc0, acc1)
    for acc in accs:
        acc[...] = jnp.zeros_like(acc)
    for copy in copies:
        copy.wait()
    for p, mask in enumerate((0, 1, 3, 2)):
        sums = []
        for b, side in itertools.product(range(UP_KEPT), range(2)):
            cell = note_ref[side, p, b]
            i, c = cell // 12, cell % 12
            left = pl.multiple_of(i * BLOCK, BLOCK)
            block = weights[side][p][8 * b : 8 * b + 8].reshape(BLOCK, BLOCK)
            some = acts[zh ^ mask, :, :, :, pl.ds(left, BLOCK)].reshape(2 * BLOCK, BLOCK)
            sums.append((side, c, jnp.dot(some, block, preferred_element_type=f32)))
        for side, c, more in sums:
            accs[side][c] += more

    def write(ref, n, side, mask):
        top = pl.multiple_of((y ^ mask) * 64, 64)
        for c in range(12):
            ref[n, :, c * BLOCK : (c + 1) * BLOCK] = accs[side][c, pl.ds(top, 64), :].astype(ref.dtype)

    write(to_near, 0, 0, 1)
    write(to_near, 1, 0, 2)
    write(to_far, 0, 1, 3)
    write(to_far, 1, 1, 2)
    write(keep, 0, 0, 0)
    write(keep, 1, 1, 0)
    write(keep, 2, 0, 3)
    write(keep, 3, 1, 1)


def up(at, notes, weights, tokens):
    smem = pl.BlockSpec(memory_space=pltpu.SMEM)
    vmem = pl.BlockSpec(memory_space=pltpu.VMEM)
    hbm = pl.BlockSpec(memory_space=pl.ANY)
    return pl.pallas_call(
        up_kernel,
        out_shape=[
            jax.ShapeDtypeStruct((2, 64, 12 * BLOCK), bf16),
            jax.ShapeDtypeStruct((2, 64, 12 * BLOCK), bf16),
            jax.ShapeDtypeStruct((4, 64, 12 * BLOCK), f32),
        ],
        in_specs=[smem, smem] + [vmem] * 8 + [hbm] * 5,
        out_specs=[vmem] * 3,
        scratch_shapes=[
            pltpu.VMEM((4, 2, 4, 32, 6 * BLOCK), bf16),
            pltpu.VMEM((12, 2 * BLOCK, BLOCK), f32),
            pltpu.VMEM((12, 2 * BLOCK, BLOCK), f32),
            pltpu.SemaphoreType.DMA((32,)),
        ],
        compiler_params=pltpu.CompilerParams(vmem_limit_bytes=VMEM_LIMIT),
    )(at, notes, *weights, *tokens)


def down_kernel(at_ref, note_ref, *refs):
    weights, hidden, (to_near, to_far, keep) = refs[:2], refs[2:7], refs[7:10]
    acts, acc0, acc1, sems = refs[10:]
    core, y = at_ref[2], at_ref[4]
    copies = []
    for n, mask in enumerate((0, 1, 3, 2)):
        for side in range(2):
            part = hidden[n].at[side] if mask != 2 else hidden[3 + side].at[0]
            copies.append(pltpu.make_async_copy(part, acts.at[y ^ mask, side], sems.at[len(copies)]))
    for copy in copies:
        copy.start()
    accs = (acc0, acc1)
    for acc in accs:
        acc[...] = jnp.zeros_like(acc)
    for copy in copies:
        copy.wait()
    over = jnp.min(acts[:, 0, 0:16, 0:BLOCK].astype(f32)) < 0.0
    for source in range(4):

        def step(group, _):
            sums = []
            for n, side in itertools.product(range(6), range(2)):
                b = 6 * group + n
                name = note_ref[side, source, b]
                of = (name >= 72).astype(jnp.int32)
                cell = name - 72 * of
                i, c = cell // 6, cell % 6
                left = pl.multiple_of(i * BLOCK, BLOCK)
                block = weights[side][source, pl.ds(8 * b, 8)].reshape(BLOCK, BLOCK)
                some = acts[:, of ^ core, :, pl.ds(left, BLOCK)].reshape(2 * BLOCK, BLOCK)
                sums.append((side, source * 6 + c, jnp.dot(some, block, preferred_element_type=f32)))
            for side, c, more in sums:
                accs[side][c] += more
            return 0

        most = jnp.maximum(note_ref[0, source, BLOCK - 1], note_ref[1, source, BLOCK - 1])
        lax.fori_loop(0, (most + 5) // 6, step, 0)
    spoilt = jnp.where(over, jnp.nan, 0.0).astype(f32)

    def write(ref, n, half, p):
        top = half * BLOCK + 32 * p
        for target, c in itertools.product(range(4), range(6)):
            total = acc0[target * 6 + c, top : top + 32, :] + acc1[target * 6 + c, top : top + 32, :] + spoilt
            ref[n, target, :, c * BLOCK : (c + 1) * BLOCK] = total.astype(ref.dtype)

    write(to_near, 0, 0, 1)
    write(to_near, 1, 0, 3)
    write(to_far, 0, 1, 2)
    write(to_far, 1, 1, 3)
    write(keep, 0, 0, 0)
    write(keep, 1, 1, 0)
    write(keep, 2, 0, 2)
    write(keep, 3, 1, 1)


def down(at, notes, weights, hidden):
    smem = pl.BlockSpec(memory_space=pltpu.SMEM)
    vmem = pl.BlockSpec(memory_space=pltpu.VMEM)
    hbm = pl.BlockSpec(memory_space=pl.ANY)
    return pl.pallas_call(
        down_kernel,
        out_shape=[
            jax.ShapeDtypeStruct((2, 4, 32, 6 * BLOCK), bf16),
            jax.ShapeDtypeStruct((2, 4, 32, 6 * BLOCK), bf16),
            jax.ShapeDtypeStruct((4, 4, 32, 6 * BLOCK), f32),
        ],
        in_specs=[smem, smem, vmem, vmem] + [hbm] * 5,
        out_specs=[vmem] * 3,
        scratch_shapes=[
            pltpu.VMEM((4, 2, 64, 12 * BLOCK), bf16),
            pltpu.VMEM((24, 2 * BLOCK, BLOCK), f32),
            pltpu.VMEM((24, 2 * BLOCK, BLOCK), f32),
            pltpu.SemaphoreType.DMA((8,)),
        ],
        compiler_params=pltpu.CompilerParams(vmem_limit_bytes=VMEM_LIMIT),
    )(at, notes, *weights, *hidden)


def body(tokens, up_weight, up_mask, up_bias, down_weight, down_mask, down_bias):
    at = jnp.stack([lax.axis_index(axis) for axis in AXES]).astype(jnp.int32)

    z = ("zh", "zl")
    rows = tokens.reshape(4, 1, 32, 6 * BLOCK)
    own = spread(jnp.broadcast_to(rows, (4, 2, 32, 6 * BLOCK)).reshape(8, 32, 6 * BLOCK), z)
    own = own.reshape(4, 2, 32, 6 * BLOCK)
    up_own = pack_up(up_mask, down_mask, up_weight)
    biases = jnp.stack([up_bias, swap_core(up_bias)])
    other_down, other_mask = swap_core(down_weight), swap_core(down_mask)

    up_mine = [up_own] + [send(up_own, flip("zh", mask)) for mask in (1, 3, 2)]
    near, far = ring_first(own, "x")
    down_packed = pack_down(at, down_mask, other_mask, down_mask, other_mask, down_weight, other_down)
    near, far, down_packed = together(near, far, down_packed)
    left, right = ring_second(near, far, "x")
    up_other = [swap_core(pack) for pack in up_mine]
    up_mine, left, right, down_packed, biases = together(up_mine, left, right, down_packed, biases)

    down_mine = spread(down_packed)
    up_packs = up_mine + up_other
    up_notes = jnp.stack([pack[8 * UP_KEPT, 0] for pack in up_packs]).astype(jnp.int32).reshape(2, 4, BLOCK)
    to_near, to_far, keep = up(at, up_notes, up_packs, [own, near, far, left, right])

    near, far = sum_first(to_near, to_far, "y")
    near, far = together(near, far)
    last, first = sum_second(near, far, keep, "y")
    sums = jnp.stack(summed(keep, near, far, last, first))
    hidden = jnp.maximum(sums + biases[:, None, :], 0.0).astype(bf16)
    over = jnp.max(up_notes[0, :, BLOCK - 2] + up_notes[1, :, BLOCK - 2]) > 2 * PAIR
    marked = jnp.where(over, -jnp.ones_like(hidden), hidden)
    near, far = ring_first(marked, "y")
    near, far = together(near, far)
    left, right = ring_second(near, far, "y")
    left, right, down_mine = together(left, right, down_mine)

    down_other = swap_core(down_mine)
    down_notes = notes_of(down_mine, down_other, PAIR)
    to_near, to_far, keep = down(at, down_notes, [down_mine, down_other], [marked, near, far, left, right])

    def place(*sums):
        pieces = jnp.stack(sums, axis=1).astype(bf16).reshape(8, 32, 6 * BLOCK)
        got = spread(pieces, z).reshape(4, 2, 32, 6 * BLOCK).astype(f32)
        return (got[:, 0] + got[:, 1] + down_bias).astype(bf16).reshape(BLOCK, 6 * BLOCK)

    near, far = sum_first(to_near, to_far, "x")
    last, first = sum_second(near, far, keep, "x")
    out = place(*summed(keep, near, far, last, first))

    def whole(_):
        kept = lax.all_gather(expand_mask(down_mask, down_weight), "zh")
        kept = jnp.stack([kept, swap_core(kept)]).transpose(0, 2, 1, 3).reshape(24 * BLOCK, 24 * BLOCK)
        acts = lax.all_gather(hidden, "y").transpose(0, 2, 1, 3).reshape(2 * BLOCK, 24 * BLOCK)
        sums = jnp.dot(acts, kept, preferred_element_type=f32).reshape(2, 4, 32, 4, 6 * BLOCK)
        x = lax.axis_index("x")
        order = jnp.array([0, 1, 3, 2])[x ^ jnp.arange(4)]
        sums = lax.psum(jnp.take(sums, order, axis=1), "x")
        sums = lax.dynamic_index_in_dim(sums, x, 1, keepdims=False).transpose(0, 2, 1, 3)
        return place(sums[0], sums[1])

    return lax.cond(jnp.isnan(out[0, 0]), whole, lambda _: out, 0)


def solution(mesh):
    fine = Mesh(mesh.devices.reshape(SIZES), AXES)
    in_specs = (P(ROW, COL), P(COL, ROW), P(COL, ROW), P(ROW), P(ROW, COL), P(ROW, COL), P(COL))
    return jax.shard_map(body, mesh=fine, in_specs=in_specs, out_specs=P(ROW, COL), check_vma=False)
```
